256 devices in a mesh: expert: 4 (over z_hi), grid: 16 (over x, z_lo, core), layer: 4 (over y).
Axes of the slice: x: 4, y: 4, z: 8 (z_hi: 4, z_lo: 2; z = z_hi * 2 + z_lo), core: 2. Of those that a mesh axis runs over, the one named last changes fastest.
Arguments:
- iterate: bfloat16 [12288, 8192], P(('expert', 'grid'), 'layer'), parts along dimension 0, may hold values from -6 to 6
Outputs:
- new_iterate: bfloat16 [12288, 8192], P(('expert', 'grid'), 'layer'), parts along dimension 0
The draws below stay inside these ranges and needn't reach their ends.
There are 4 independent parts, one for each index of `expert`. The reference program is written for one: setup_inputs(seed, part) draws one part's arguments, and reference() takes and returns one part's arrays. A program takes and returns all parts, laid end to end along the dimension named above; each array names one. Nothing has to cross between parts.
All inputs are finite; a program needn't handle non-finite values.
Results may differ from the reference program's by a relative error of at most 0.03.
Values may be sent and summed in bfloat16 or wider, within the bound.
A program may use at most 64 MiB of HBM per device.

```python
import jax
import jax.numpy as jnp
from jax import lax

M = 3072
N = 8192
N_LAYER = 4


def levels(stream_key, dims, split, least, high):
    factor_of, own = 1.0, jax.random.fold_in(stream_key, 6)
    for axis_at, shards_of in split:
        steps = jnp.exp(jax.random.uniform(jax.random.fold_in(own, axis_at), (shards_of,), jnp.float32, least / len(split), high / len(split)))
        factor_of = factor_of * jnp.repeat(steps, dims[axis_at] // shards_of).reshape([-1 if axis == axis_at else 1 for axis in range(len(dims))])
    return factor_of


def scatter_about(key, extent, deviation, limit, pieces=(), dtype=jnp.bfloat16):
    result = jax.random.normal(key, extent, jnp.float32) * deviation
    if len(pieces) > 0:
        result = levels(key, extent, pieces, -0.22, 0.18) * result
    return jnp.clip(result, min=-limit, max=limit).astype(dtype)


def setup_inputs(seed: int = 0, part: int = 0) -> dict:
    streams_of = jax.random.split(jax.random.key(seed), 2)
    part_splits = jax.random.split(jax.random.fold_in(streams_of[1], part), 2)
    iterate = scatter_about(part_splits[0], (M, N), 0.7, 6.0, ((0, 16), (1, 4)))
    return dict(iterate=iterate)


linear_coef = 3.4445
cubic_coef = -4.7750
quintic_coef = 2.0315


def rounded(value):
    low = lax.optimization_barrier(value.astype(jnp.bfloat16))
    return low.astype(jnp.float32)


def reference(iterate):
    col_width = N // N_LAYER
    quarter = M // N_LAYER
    gram_sum = jnp.zeros((M, M), jnp.float32)
    for layer_idx in range(N_LAYER):
        column_block = iterate[:, layer_idx * col_width:(layer_idx + 1) * col_width]
        partial_value = jnp.dot(column_block, column_block.T, preferred_element_type=jnp.float32) * (1.0 / N)
        gram_sum = gram_sum + rounded(partial_value)
    gram_low = gram_sum.astype(jnp.bfloat16)
    square = jnp.zeros((M, M), jnp.float32)
    for layer_idx in range(N_LAYER):
        gram_cols = gram_low[:, layer_idx * quarter:(layer_idx + 1) * quarter]
        partial_value = jnp.dot(gram_cols, gram_cols.T, preferred_element_type=jnp.float32)
        square = square + rounded(partial_value)
    mixed = (cubic_coef * gram_sum + quintic_coef * square).astype(jnp.bfloat16)
    product = jnp.dot(mixed, iterate, preferred_element_type=jnp.float32)
    return (linear_coef * iterate.astype(jnp.float32) + product).astype(jnp.bfloat16)
```

```python
import functools

import jax
import jax.numpy as jnp
from jax import lax
from jax.experimental import pallas as pl
from jax.experimental.pallas import tpu as pltpu
from jax.sharding import PartitionSpec as P

MESH = pl.DeviceIdType.MESH

LINEAR = 3.4445
CUBIC = -4.775
QUINTIC = 2.0315

NX = 4
NY = 4
SHIFTS = (0, 1, 3, 2)
CHUNKS = 3


def kernel(n_cols, x_ref, o_ref, rows, send, part, got, gram, g32, sq, sgot, mixed, ypart, yrem, ssem, rsem, lsem):
    half, width = x_ref.shape[0] // 2, x_ref.shape[1]
    quarter = half
    chunk = quarter // CHUNKS
    block = 4 * half
    expert, grid, y = lax.axis_index("expert"), lax.axis_index("grid"), lax.axis_index("layer")
    x, z, c = grid // 4, (grid // 2) % 2, grid % 2
    home = c == z

    def at(x_to=None, z_to=None, c_to=None, y_to=None):
        gx = x if x_to is None else x_to
        gz = z if z_to is None else z_to
        gc = c if c_to is None else c_to
        return (expert, gx * 4 + gz * 2 + gc, y if y_to is None else y_to)

    def around(base, step):
        return (base + step) % 4

    right, left = at(x_to=around(x, 1)), at(x_to=around(x, 3))
    sibling = at(c_to=1 - c)
    across = at(z_to=1 - z, c_to=z)
    along_y = [at(y_to=around(y, step)) for step in (1, 2, 3)]

    barrier = pltpu.get_barrier_semaphore()
    greeted = [right, left, sibling, at(z_to=1 - z), at(z_to=1 - z, c_to=1 - c)] + along_y
    for device in greeted:
        pl.semaphore_signal(barrier, inc=1, device_id=device, device_id_type=MESH)
    pl.semaphore_wait(barrier, len(greeted))

    used = [0, 0]
    pending = []

    def slots(count=1):
        used[1] += count
        return used[1] - count

    def copy(src, dst, device, slot):
        used[0] += 1
        made = pltpu.make_async_remote_copy(
            src_ref=src, dst_ref=dst, send_sem=ssem.at[used[0] - 1], recv_sem=rsem.at[slot],
            device_id=device, device_id_type=MESH,
        )
        return made

    def push(src, dst, device, slot=None):
        made = copy(src, dst, device, slots() if slot is None else slot)
        made.start()
        pending.append(made)
        return made

    def x_block(core_half):
        return x_ref.at[pl.ds(core_half * half, half), :]

    from_left = [None, None]
    from_right = [None, None]
    for piece in (0, 1):
        from_left[piece] = push(x_block(piece), rows.at[x, c, piece], right)
        from_right[1 - piece] = push(x_block(1 - piece), rows.at[x, c, 1 - piece], left)
    z_slot = slots(4)
    for piece in (0, 1):
        push(x_block(piece), rows.at[4, c, piece], across, z_slot + 2 * c + piece)
    own_sib = [push(x_block(piece), rows.at[x, c, piece], sibling) for piece in (0, 1)]
    own = [pltpu.make_async_copy(x_block(piece), rows.at[x, c, piece], lsem.at[piece]) for piece in (0, 1)]
    for made in own:
        made.start()
    for made in own:
        made.wait()
    for made in own_sib:
        made.wait_recv()

    mine = jnp.where(home, x, 4)
    parts = {}

    def gram_block(i):
        xp = around(x, SHIFTS[i])
        product = lax.dot_general(
            rows[mine].reshape(block, width), rows[xp].reshape(block, width),
            (((1,), (1,)), ((), ())), preferred_element_type=jnp.float32,
        )
        part[i] = (product * (1.0 / n_cols)).astype(jnp.bfloat16).reshape(4, quarter, block)

    def gram_send(i):
        parts[i] = [push(part.at[i, around(y, step)], got.at[i, step - 1], along_y[step - 1]) for step in (1, 2, 3)]

    @pl.when(home)
    def _():
        gram_block(0)

    xl, xr, xo = around(x, 3), around(x, 1), around(x, 2)
    sib = {}
    far = [None, None]
    from_left[0].wait_recv()
    far[0] = push(rows.at[xl, c, 0], rows.at[xl, c, 0], right)
    sib[(3, 0)] = push(rows.at[xl, c, 0], rows.at[xl, c, 0], sibling)
    from_right[1].wait_recv()
    far[1] = push(rows.at[xr, c, 1], rows.at[xr, c, 1], left)
    sib[(1, 1)] = push(rows.at[xr, c, 1], rows.at[xr, c, 1], sibling)
    from_left[1].wait_recv()
    sib[(3, 1)] = push(rows.at[xl, c, 1], rows.at[xl, c, 1], sibling)
    from_right[0].wait_recv()
    sib[(1, 0)] = push(rows.at[xr, c, 0], rows.at[xr, c, 0], sibling)

    @pl.when(jnp.logical_not(home))
    def _():
        for k in range(4):
            pltpu.make_async_remote_copy(
                src_ref=x_block(0), dst_ref=rows.at[4, k // 2, k % 2], send_sem=ssem.at[0],
                recv_sem=rsem.at[z_slot + k], device_id=sibling, device_id_type=MESH,
            ).wait_recv()
        gram_block(0)

    gram_send(0)
    for i in (1, 2):
        for piece in (0, 1):
            sib[(SHIFTS[i], piece)].wait_recv()
        gram_block(i)
        gram_send(i)
    for piece in (0, 1):
        far[piece].wait_recv()
        sib[(2, piece)] = push(rows.at[xo, c, piece], rows.at[xo, c, piece], sibling)
    for piece in (0, 1):
        sib[(2, piece)].wait_recv()
    gram_block(3)
    gram_send(3)

    to_right, to_left, gsib = [], [], []
    zg_slot = slots(8)

    def push_across(i, xs):
        push(gram.at[x, xs, c], gram.at[4, xs, c], across, zg_slot + 2 * i + c)

    for i in range(4):
        for made in parts[i]:
            made.wait_recv()
        xp = around(x, SHIFTS[i])
        total = part[i, y].astype(jnp.float32)
        for step in range(3):
            total += got[i, step].astype(jnp.float32)
        g32[xp] = total
        gram[xp, x, c] = total.astype(jnp.bfloat16)
        to_right.append(push(gram.at[xp, x, c], gram.at[xp, x, c], right))
        to_left.append(push(gram.at[xp, x, c], gram.at[xp, x, c], left))
        gsib.append(push(gram.at[xp, x, c], gram.at[xp, x, c], sibling))
        if i == 0:
            push_across(0, x)

    gfar = []
    for i in range(4):
        for made, xs, onward, keep in ((to_right[i], xl, right, i in (0, 2)), (to_left[i], xr, left, i in (1, 3))):
            made.wait_recv()
            xp = around(xs, SHIFTS[i])
            ref = gram.at[xp, xs, c]
            if keep:
                gfar.append((i, push(ref, ref, onward)))
            if xs is xl and SHIFTS[i] == 1 or xs is xr and SHIFTS[i] == 3:
                push_across(1 if xs is xl else 2, xs)
            gsib.append(push(ref, ref, sibling))
    for i, made in gfar:
        made.wait_recv()
        ref = gram.at[around(xo, SHIFTS[i]), xo, c]
        if SHIFTS[i] == 2:
            push_across(3, xo)
        gsib.append(push(ref, ref, sibling))
    for made in gsib:
        made.wait_recv()

    @pl.when(jnp.logical_not(home))
    def _():
        for k in range(8):
            pltpu.make_async_remote_copy(
                src_ref=gram.at[0, 0, 0], dst_ref=gram.at[4, k // 2, k % 2], send_sem=ssem.at[0],
                recv_sem=rsem.at[zg_slot + k], device_id=sibling, device_id_type=MESH,
            ).wait_recv()

    first = gram[mine].reshape(2 * block, block).T
    for xp in range(4):
        sq[:, :, :, xp * block:(xp + 1) * block] = jnp.dot(
            first, gram[xp].reshape(2 * block, block), preferred_element_type=jnp.float32
        ).astype(jnp.bfloat16).reshape(4, CHUNKS, chunk, block)

    squares = []
    for k in range(CHUNKS):
        squares.append([push(sq.at[around(y, step), k], sgot.at[k, step - 1], along_y[step - 1]) for step in (1, 2, 3)])

    gathers = []

    def mix(k):
        for made in squares[k]:
            made.wait_recv()
        total = sq[y, k].astype(jnp.float32)
        for step in range(3):
            total += sgot[k, step].astype(jnp.float32)
        g = jnp.concatenate([g32[xp, k * chunk:(k + 1) * chunk, :] for xp in range(4)], axis=1)
        mixed[k, y] = (CUBIC * g + QUINTIC * total).astype(jnp.bfloat16)
        gathers.append([push(mixed.at[k, y], mixed.at[k, y], device) for device in along_y])

    y_slot, s_slot = slots(CHUNKS), slots(CHUNKS)
    y_sends, s_sends = [], []

    def multiply(k):
        for made in gathers[k]:
            made.wait_recv()
        lhs = mixed[k].reshape(4 * chunk, 4 * block)
        tile = width // 4
        for t in range(4):
            ypart[k, :, :, :, t * tile:(t + 1) * tile] = jnp.dot(
                lhs, rows[:4, :, :, :, t * tile:(t + 1) * tile].reshape(4 * block, tile), preferred_element_type=jnp.float32
            ).astype(jnp.bfloat16).reshape(2, 2, chunk, tile)
        away = [copy(ypart.at[k, h], yrem.at[0, k], at(z_to=1 - z, c_to=h), y_slot + k) for h in (0, 1)]
        near = copy(ypart.at[k, 1 - c], yrem.at[1, k], sibling, s_slot + k)
        y_sends.append(away)
        s_sends.append(near)

        @pl.when(home)
        def _():
            near.start()

        @pl.when(jnp.logical_not(home))
        def _():
            away[0].start()
            away[1].start()

    for k in range(CHUNKS):
        mix(k)
        if k:
            multiply(k - 1)
    multiply(CHUNKS - 1)

    for k in range(CHUNKS):
        y_sends[k][0].wait_recv()

        @pl.when(jnp.logical_not(home))
        def _():
            s_sends[k].wait_recv()

        for q in range(2):
            near = jnp.where(home, ypart[k, c, q].astype(jnp.float32), yrem[1, k, q].astype(jnp.float32))
            low = q * quarter + k * chunk
            o_ref[low:low + chunk, :] = (
                LINEAR * x_ref[low:low + chunk, :].astype(jnp.float32) + (near + yrem[0, k, q].astype(jnp.float32))
            ).astype(jnp.bfloat16)

    for made in pending:
        made.wait_send()

    @pl.when(home)
    def _():
        for made in s_sends:
            made.wait_send()

    @pl.when(jnp.logical_not(home))
    def _():
        for pair in y_sends:
            for made in pair:
                made.wait_send()


def body(n_cols, iterate):
    height, width = iterate.shape
    half = height // 2
    block = 2 * height
    chunk = half // CHUNKS
    bf16 = jnp.bfloat16
    return pl.pallas_call(
        functools.partial(kernel, n_cols),
        out_shape=jax.ShapeDtypeStruct(iterate.shape, bf16),
        in_specs=[pl.BlockSpec(memory_space=pltpu.VMEM)],
        out_specs=pl.BlockSpec(memory_space=pltpu.VMEM),
        scratch_shapes=[
            pltpu.VMEM((5, 2, 2, half, width), bf16),
            pltpu.VMEM((8, 128), bf16),
            pltpu.VMEM((4, 4, half, block), bf16),
            pltpu.VMEM((4, 3, half, block), bf16),
            pltpu.VMEM((5, 4, 2, half, block), bf16),
            pltpu.VMEM((4, half, block), jnp.float32),
            pltpu.VMEM((4, CHUNKS, chunk, 4 * block), bf16),
            pltpu.VMEM((CHUNKS, 3, chunk, 4 * block), bf16),
            pltpu.VMEM((CHUNKS, 4, chunk, 4 * block), bf16),
            pltpu.VMEM((CHUNKS, 2, 2, chunk, width), bf16),
            pltpu.VMEM((2, CHUNKS, 2, chunk, width), bf16),
            pltpu.SemaphoreType.DMA((128,)),
            pltpu.SemaphoreType.DMA((128,)),
            pltpu.SemaphoreType.DMA((2,)),
        ],
        compiler_params=pltpu.CompilerParams(
            collective_id=0, has_side_effects=True, vmem_limit_bytes=60 * 2**20
        ),
        cost_estimate=pl.CostEstimate(flops=6 * 10**9, bytes_accessed=2 * 10**6, transcendentals=0),
        name="newton_schulz",
    )(iterate)


def solution(mesh):
    spec = P(("expert", "grid"), "layer")

    def run(iterate):
        step = functools.partial(body, iterate.shape[1])
        return jax.shard_map(step, mesh=mesh, in_specs=(spec,), out_specs=spec, check_vma=False)(iterate)

    return run
```

```python
import functools

import jax
import jax.numpy as jnp
from jax import lax
from jax.experimental import pallas as pl
from jax.experimental.pallas import tpu as pltpu
from jax.sharding import PartitionSpec as P

MESH = pl.DeviceIdType.MESH

LINEAR = 3.4445
CUBIC = -4.775
QUINTIC = 2.0315

SHIFTS = (0, 1, 3, 2)
CHUNKS = 3
AHEAD = 1
HOLD = 0
PASS_AT = 3


def kernel(
    n_cols, x_ref, o_ref, rows, part, pgot, gram, g32, sq, srel, sacc, sgot, mloc, mixed, ssem, rsem, lsem
):
    half, width = x_ref.shape[0] // 2, x_ref.shape[1]
    quarter = half
    half_q = quarter // 2
    chunk = quarter // CHUNKS
    block = 4 * half
    expert, grid, y = lax.axis_index("expert"), lax.axis_index("grid"), lax.axis_index("layer")
    x, z, c = grid // 4, (grid // 2) % 2, grid % 2
    home = c == z
    visitor = jnp.logical_not(home)

    def at(x_to=None, z_to=None, c_to=None, y_to=None):
        gx = x if x_to is None else x_to
        gz = z if z_to is None else z_to
        gc = c if c_to is None else c_to
        return (expert, gx * 4 + gz * 2 + gc, y if y_to is None else y_to)

    def around(base, step):
        return (base + step) % 4

    up, down, opposite = around(y, 1), around(y, 3), around(y, 2)
    xl, xr, xo = around(x, 3), around(x, 1), around(x, 2)
    right, left = at(x_to=xr), at(x_to=xl)
    sibling = at(c_to=1 - c)
    beyond = at(z_to=1 - z)
    across = at(z_to=1 - z, c_to=z)
    to_up, to_down = at(y_to=up), at(y_to=down)
    taker = y // 2

    barrier = pltpu.get_barrier_semaphore()
    greeted = [right, left, sibling, beyond, at(z_to=1 - z, c_to=1 - c), to_up, to_down]
    greeted += [at(c_to=1 - c, y_to=up), at(c_to=1 - c, y_to=down), at(y_to=opposite), at(x_to=xo)]
    for device in greeted:
        pl.semaphore_signal(barrier, inc=1, device_id=device, device_id_type=MESH)
    pl.semaphore_wait(barrier, len(greeted))

    used = [0, 0]
    pending = []
    guarded = []

    def slots(count=1):
        used[1] += count
        return used[1] - count

    def copy(src, dst, device, slot=None):
        used[0] += 1
        return pltpu.make_async_remote_copy(
            src_ref=src, dst_ref=dst, send_sem=ssem.at[used[0] - 1],
            recv_sem=rsem.at[slots() if slot is None else slot], device_id=device, device_id_type=MESH,
        )

    def push(src, dst, device, slot=None):
        made = copy(src, dst, device, slot)
        made.start()
        pending.append(made)
        return made

    def push_if(condition, copies):
        guarded.append((condition, copies))

        @pl.when(condition)
        def _():
            for made in copies:
                made.start()

    def arrive(ref, slot):
        pltpu.make_async_remote_copy(
            src_ref=ref, dst_ref=ref, send_sem=ssem.at[0], recv_sem=rsem.at[slot],
            device_id=sibling, device_id_type=MESH,
        ).wait_recv()

    def arrive_if(condition, copies):
        @pl.when(condition)
        def _():
            for made in copies:
                made.wait_recv()

    def x_block(core_half):
        return x_ref.at[pl.ds(core_half * half, half), :]

    from_left = [None, None]
    from_right = [None, None]
    for piece in (0, 1):
        from_left[piece] = push(x_block(piece), rows.at[x, c, piece], right)
        from_right[1 - piece] = push(x_block(1 - piece), rows.at[x, c, 1 - piece], left)
    z_slot = slots(4)
    for piece in (0, 1):
        push(x_block(piece), rows.at[4 + x, c, piece], across, z_slot + 2 * c + piece)
    own_sib = [push(x_block(piece), rows.at[x, c, piece], sibling) for piece in (0, 1)]
    own = [pltpu.make_async_copy(x_block(piece), rows.at[x, c, piece], lsem.at[piece]) for piece in (0, 1)]
    for made in own:
        made.start()
    for made in own:
        made.wait()
    for made in own_sib:
        made.wait_recv()

    mine = jnp.where(home, x, 4 + x)

    def gram_block(i):
        xp = around(x, SHIFTS[i])
        product = lax.dot_general(
            rows[mine].reshape(block, width), rows[xp].reshape(block, width),
            (((1,), (1,)), ((), ())), preferred_element_type=jnp.float32,
        )
        part[i] = (product * (1.0 / n_cols)).astype(jnp.bfloat16).reshape(4, quarter, block)

    head, tail = pl.ds(0, half_q), pl.ds(half_q, half_q)
    parts = {}
    for i in range(4):
        parts[i] = [copy(part.at[i, to], pgot.at[i, k], at(y_to=to)) for k, to in enumerate((opposite, up, down))]
        pending.extend(parts[i])

    def gram_send(i):
        for made in parts[i]:
            made.start()

    @pl.when(home)
    def _():
        gram_block(0)
        gram_send(0)

    sib = {}
    far = [None, None]
    from_left[0].wait_recv()
    far[0] = push(rows.at[xl, c, 0], rows.at[xl, c, 0], right)
    sib[(3, 0)] = push(rows.at[xl, c, 0], rows.at[xl, c, 0], sibling)
    from_right[1].wait_recv()
    far[1] = push(rows.at[xr, c, 1], rows.at[xr, c, 1], left)
    sib[(1, 1)] = push(rows.at[xr, c, 1], rows.at[xr, c, 1], sibling)
    from_left[1].wait_recv()
    sib[(3, 1)] = push(rows.at[xl, c, 1], rows.at[xl, c, 1], sibling)
    from_right[0].wait_recv()
    sib[(1, 0)] = push(rows.at[xr, c, 0], rows.at[xr, c, 0], sibling)
    later_z = [push(rows.at[xp, c, piece], rows.at[4 + xp, c, piece], beyond) for xp, piece in ((xl, 0), (xr, 1))]
    to_home = [copy(rows.at[4 + x], rows.at[4 + x], sibling)]

    @pl.when(visitor)
    def _():
        for k in range(4):
            arrive(rows.at[4 + x, k // 2, k % 2], z_slot + k)
        gram_block(0)
        gram_send(0)

    for i in (1, 2):
        for piece in (0, 1):
            sib[(SHIFTS[i], piece)].wait_recv()
        gram_block(i)
        gram_send(i)
    push_if(visitor, to_home)
    for piece in (0, 1):
        far[piece].wait_recv()
        sib[(2, piece)] = push(rows.at[xo, c, piece], rows.at[xo, c, piece], sibling)
    for piece in (0, 1):
        sib[(2, piece)].wait_recv()
    gram_block(3)
    gram_send(3)

    to_right, to_left, gsib, gfar, direct_far = {}, {}, [], [], []
    zg_slot = slots(8)

    def total_block(i):
        for made in parts[i]:
            made.wait_recv()
        xp = around(x, SHIFTS[i])
        total = part[i, y].astype(jnp.float32)
        for k in range(3):
            total += pgot[i, k].astype(jnp.float32)
        g32[xp] = total
        gram[xp, x, c] = total.astype(jnp.bfloat16)
        ref = gram.at[xp, x, c]
        if i == 3:
            direct_far.append(push(ref, ref, at(x_to=xo)))
        to_right[i] = push(ref, ref, right)
        to_left[i] = push(ref, ref, left)
        if i == 0:
            push(ref, gram.at[4, x, c], across, zg_slot + c)
        gsib.append(push(ref, ref, sibling))

    def pass_on(i):
        for made, xs, onward, low, shift in ((to_right[i], xl, right, 0, 1), (to_left[i], xr, left, half_q, 3)):
            made.wait_recv()
            xp = around(xs, SHIFTS[i])
            ref = gram.at[xp, xs, c]
            if i < 3:
                ahead = gram.at[xp, xs, c, pl.ds(low, half_q)]
                gfar.append((i, low, push(ahead, ahead, onward)))
            if SHIFTS[i] == shift:
                push(ref, gram.at[4, xs, c], across, zg_slot + 2 * i + c)
            gsib.append(push(ref, ref, sibling))

    total_block(0)
    total_block(1)
    total_block(2)
    pass_on(0)
    pass_on(1)
    total_block(3)
    pass_on(2)
    for i, low, made in gfar:
        made.wait_recv()
        ref = gram.at[around(xo, SHIFTS[i]), xo, c, pl.ds(low, half_q)]
        gsib.append(push(ref, ref, sibling))
    pass_on(3)
    direct_far[0].wait_recv()
    ref = gram.at[x, xo, c]
    push(ref, gram.at[4, xo, c], across, zg_slot + 6 + c)
    gsib.append(push(ref, ref, sibling))

    sides = ((1, xl, right, 0), (0, xr, left, 1))
    later_x = [copy(rows.at[4 + x, :, p], rows.at[4 + x, :, p], device) for p, _, device, _ in sides]
    later_far = [copy(rows.at[4 + xs, q, p], rows.at[4 + xs, q, p], device) for p, xs, device, q in sides]
    later_home = [copy(rows.at[4 + xs, :, p], rows.at[4 + xs, :, p], sibling) for p, xs, _, _ in sides]
    last_home = [copy(rows.at[4 + xo, q, p], rows.at[4 + xo, q, p], sibling) for p, _, _, q in sides]
    push_if(visitor, later_x)
    last_z = push(rows.at[xo, c, c], rows.at[4 + xo, c, c], beyond)

    for made in gsib:
        made.wait_recv()

    @pl.when(visitor)
    def _():
        for k in range(8):
            arrive(gram.at[0, 0, 0], zg_slot + k)

    first = gram[mine - jnp.where(home, 0, x)].reshape(2 * block, block).T
    for xp in range(4):
        sq[:, :, :, xp * block:(xp + 1) * block] = jnp.dot(
            first, gram[xp].reshape(2 * block, block), preferred_element_type=jnp.float32
        ).astype(jnp.bfloat16).reshape(4, CHUNKS, chunk, block)

    later_sib = []
    for (xp, piece), made in zip(((xl, 0), (xr, 1)), later_z):
        made.wait_recv()
        later_sib.append(push(rows.at[4 + xp, c, piece], rows.at[4 + xp, c, piece], sibling))

    lane = (slice(None), pl.ds(0, 2 * block)), (slice(None), pl.ds(2 * block, 2 * block))
    relay, direct, summed = {}, {}, {}

    def scatter(k):
        relay[k] = [
            push(sq.at[opposite, k, *lane[1]], srel.at[k, 0], to_up),
            push(sq.at[opposite, k, *lane[0]], srel.at[k, 1], to_down),
        ]
        direct[k] = [
            push(sq.at[up, k, *lane[0]], sgot.at[k, 0], to_up),
            push(sq.at[down, k, *lane[1]], sgot.at[k, 1], to_down),
        ]

    def add_on(k):
        summed[k] = []
        for d, (target, device) in enumerate(((up, to_up), (down, to_down))):
            relay[k][d].wait_recv()
            own_part = sq[target, k, :, 2 * block * (1 - d):2 * block * (2 - d)]
            sacc[k, d] = (srel[k, d].astype(jnp.float32) + own_part.astype(jnp.float32)).astype(jnp.bfloat16)
            summed[k].append(push(sacc.at[k, d], sgot.at[k, 2 + d], device))

    near = (slice(None), pl.ds(0, 4 * block))
    other = (slice(None), pl.ds(4 * block, 4 * block))
    takes = c == taker
    takes_down, takes_up, takes_opposite = c == down // 2, c == up // 2, c == opposite // 2
    both = jnp.logical_and
    spread, onward = {}, {}

    def mix(k):
        for made in direct[k] + summed[k]:
            made.wait_recv()
        total = sq[y, k].astype(jnp.float32) + jnp.concatenate(
            [sgot[k, 0].astype(jnp.float32) + sgot[k, 3].astype(jnp.float32),
             sgot[k, 1].astype(jnp.float32) + sgot[k, 2].astype(jnp.float32)], axis=1)
        g = jnp.concatenate([g32[xp, k * chunk:(k + 1) * chunk, :] for xp in range(4)], axis=1)
        value = (CUBIC * g + QUINTIC * total).astype(jnp.bfloat16)
        mloc[k] = value
        src = mloc.at[k]
        spread[k] = dict(
            down_near=copy(src, mixed.at[k, y, *near], at(c_to=taker, y_to=up)),
            up_near=copy(src, mixed.at[k, y, *near], at(c_to=taker, y_to=down)),
            own_near=copy(src, mixed.at[k, y, *near], sibling),
            own_other=copy(src, mixed.at[k, y, *other], at(z_to=1 - z, c_to=taker)),
        )
        push_if(visitor, [spread[k]["own_other"]])
        push_if(home, [spread[k]["down_near"], spread[k]["up_near"]])
        push_if(both(home, jnp.logical_not(takes)), [spread[k]["own_near"]])

        @pl.when(both(home, takes))
        def _():
            mixed[k, y, :, :4 * block] = value

    def spread_other(k):
        arrive_if(takes, [spread[k]["own_other"]])
        ref = mixed.at[k, y, *other]
        onward[k] = dict(down_other=copy(ref, ref, to_up), up_other=copy(ref, ref, to_down))
        push_if(takes, [onward[k]["down_other"], onward[k]["up_other"]])

    def carry(k):
        arrive_if(takes_down, [spread[k]["down_near"]])
        ref = mixed.at[k, down, *near]
        onward[k]["far_near"] = copy(ref, ref, to_up)
        push_if(takes_down, [onward[k]["far_near"]])
        arrive_if(takes_up, [onward[k]["up_other"]])
        ref = mixed.at[k, up, *other]
        onward[k]["far_other"] = copy(ref, ref, to_down)
        push_if(takes_up, [onward[k]["far_other"]])

    def multiply(k):
        arrive_if(takes_down, [onward[k]["down_other"]])
        arrive_if(takes_up, [spread[k]["up_near"]])
        arrive_if(takes_opposite, [onward[k]["far_near"], onward[k]["far_other"]])
        arrive_if(both(takes, visitor), [spread[k]["own_near"]])
        lhs = mixed[k, pl.ds(2 * c, 2)].reshape(2 * chunk, 8 * block)
        tile = width // 4
        for t in range(4):
            cols = slice(t * tile, (t + 1) * tile)
            product = jnp.dot(
                lhs, rows[:, :, :, :, cols].reshape(8 * block, tile), preferred_element_type=jnp.float32
            )
            for q in range(2):
                low = q * quarter + k * chunk
                o_ref[low:low + chunk, cols] = (
                    LINEAR * x_ref[low:low + chunk, cols].astype(jnp.float32) + product[q * chunk:(q + 1) * chunk]
                ).astype(jnp.bfloat16)

    def pass_rows():
        for p in range(2):
            arrive_if(visitor, [later_x[p]])
            push_if(visitor, [later_far[p], later_home[p]])
        last_z.wait_recv()
        later_sib.append(push(rows.at[4 + xo, c, c], rows.at[4 + xo, c, c], sibling))

    def end_rows():
        for p in range(2):
            arrive_if(visitor, [later_far[p]])
            push_if(visitor, [last_home[p]])
        for made in later_sib:
            made.wait_recv()
        arrive_if(home, to_home + later_home + last_home)

    stages = (
        (scatter, 0), (add_on, AHEAD), (mix, AHEAD + 1), (spread_other, AHEAD + 2), (carry, AHEAD + 3),
        (multiply, AHEAD + 4 + HOLD),
    )
    for slot in range(CHUNKS + AHEAD + 4 + HOLD):
        if slot == PASS_AT:
            pass_rows()
        for stage, delay in stages:
            if stage is multiply and slot == delay:
                end_rows()
            if 0 <= slot - delay < CHUNKS:
                stage(slot - delay)

    for made in pending:
        made.wait_send()
    for condition, copies in guarded:

        @pl.when(condition)
        def _():
            for made in copies:
                made.wait_send()


def body(n_cols, iterate):
    height, width = iterate.shape
    half = height // 2
    block = 2 * height
    chunk = half // CHUNKS
    bf16 = jnp.bfloat16
    return pl.pallas_call(
        functools.partial(kernel, n_cols),
        out_shape=jax.ShapeDtypeStruct(iterate.shape, bf16),
        in_specs=[pl.BlockSpec(memory_space=pltpu.VMEM)],
        out_specs=pl.BlockSpec(memory_space=pltpu.VMEM),
        scratch_shapes=[
            pltpu.VMEM((8, 2, 2, half, width), bf16),
            pltpu.VMEM((4, 4, half, block), bf16),
            pltpu.VMEM((4, 3, half, block), bf16),
            pltpu.VMEM((5, 4, 2, half, block), bf16),
            pltpu.VMEM((4, half, block), jnp.float32),
            pltpu.VMEM((4, CHUNKS, chunk, 4 * block), bf16),
            pltpu.VMEM((CHUNKS, 2, chunk, 2 * block), bf16),
            pltpu.VMEM((CHUNKS, 2, chunk, 2 * block), bf16),
            pltpu.VMEM((CHUNKS, 4, chunk, 2 * block), bf16),
            pltpu.VMEM((CHUNKS, chunk, 4 * block), bf16),
            pltpu.VMEM((CHUNKS, 4, chunk, 8 * block), bf16),
            pltpu.SemaphoreType.DMA((256,)),
            pltpu.SemaphoreType.DMA((256,)),
            pltpu.SemaphoreType.DMA((2,)),
        ],
        compiler_params=pltpu.CompilerParams(
            collective_id=0, has_side_effects=True, vmem_limit_bytes=60 * 2**20
        ),
        cost_estimate=pl.CostEstimate(flops=6 * 10**9, bytes_accessed=2 * 10**6, transcendentals=0),
        name="newton_schulz",
    )(iterate)


def solution(mesh):
    spec = P(("expert", "grid"), "layer")

    def run(iterate):
        step = functools.partial(body, iterate.shape[1])
        return jax.shard_map(step, mesh=mesh, in_specs=(spec,), out_specs=spec, check_vma=False)(iterate)

    return run
```

```python
import functools

import jax
import jax.numpy as jnp
from jax import lax
from jax.experimental import pallas as pl
from jax.experimental.pallas import tpu as pltpu
from jax.sharding import PartitionSpec as P

MESH = pl.DeviceIdType.MESH

LINEAR = 3.4445
CUBIC = -4.775
QUINTIC = 2.0315

SHIFTS = (0, 1, 3, 2)
CHUNKS = 3
AHEAD = 1
HOLD = 0
PASS_AT = 3


def kernel(
    n_cols, x_ref, o_ref, rows, part, pgot, gram, g32, sq, srel, sacc, sgot, mloc, mixed, result, ssem, rsem, lsem
):
    half, width = x_ref.shape[0] // 2, x_ref.shape[1]
    quarter = half
    half_q = quarter // 2
    chunk = quarter // CHUNKS
    block = 4 * half
    expert, grid, y = lax.axis_index("expert"), lax.axis_index("grid"), lax.axis_index("layer")
    x, z, c = grid // 4, (grid // 2) % 2, grid % 2
    home = c == z
    visitor = jnp.logical_not(home)

    def at(x_to=None, z_to=None, c_to=None, y_to=None):
        gx = x if x_to is None else x_to
        gz = z if z_to is None else z_to
        gc = c if c_to is None else c_to
        return (expert, gx * 4 + gz * 2 + gc, y if y_to is None else y_to)

    def around(base, step):
        return (base + step) % 4

    up, down, opposite = around(y, 1), around(y, 3), around(y, 2)
    xl, xr, xo = around(x, 3), around(x, 1), around(x, 2)
    right, left = at(x_to=xr), at(x_to=xl)
    sibling = at(c_to=1 - c)
    beyond = at(z_to=1 - z)
    across = at(z_to=1 - z, c_to=z)
    to_up, to_down = at(y_to=up), at(y_to=down)
    taker = y // 2

    def x_block(core_half):
        return x_ref.at[pl.ds(core_half * half, half), :]

    own = [pltpu.make_async_copy(x_block(piece), rows.at[x, c, piece], lsem.at[piece]) for piece in (0, 1)]
    for made in own:
        made.start()

    barrier = pltpu.get_barrier_semaphore()
    greeted = [right, left, sibling, beyond, at(z_to=1 - z, c_to=1 - c), to_up, to_down]
    greeted += [at(c_to=1 - c, y_to=up), at(c_to=1 - c, y_to=down), at(y_to=opposite), at(x_to=xo)]
    greeted += [at(z_to=1 - z, c_to=core, y_to=to) for core in (0, 1) for to in (up, down)]
    for device in greeted:
        pl.semaphore_signal(barrier, inc=1, device_id=device, device_id_type=MESH)
    pl.semaphore_wait(barrier, len(greeted))

    used = [0, 0]
    pending = []
    guarded = []

    def slots(count=1):
        used[1] += count
        return used[1] - count

    def copy(src, dst, device, slot=None):
        used[0] += 1
        return pltpu.make_async_remote_copy(
            src_ref=src, dst_ref=dst, send_sem=ssem.at[used[0] - 1],
            recv_sem=rsem.at[slots() if slot is None else slot], device_id=device, device_id_type=MESH,
        )

    def push(src, dst, device, slot=None):
        made = copy(src, dst, device, slot)
        made.start()
        pending.append(made)
        return made

    def push_if(condition, copies):
        guarded.append((condition, copies))

        @pl.when(condition)
        def _():
            for made in copies:
                made.start()

    def arrive(ref, slot):
        pltpu.make_async_remote_copy(
            src_ref=ref, dst_ref=ref, send_sem=ssem.at[0], recv_sem=rsem.at[slot],
            device_id=sibling, device_id_type=MESH,
        ).wait_recv()

    def arrive_if(condition, copies):
        @pl.when(condition)
        def _():
            for made in copies:
                made.wait_recv()

    from_left = [None, None]
    from_right = [None, None]
    for piece in (0, 1):
        from_left[piece] = push(x_block(piece), rows.at[x, c, piece], right)
        from_right[1 - piece] = push(x_block(1 - piece), rows.at[x, c, 1 - piece], left)
    z_slot = slots(4)
    for piece in (0, 1):
        push(x_block(piece), rows.at[4 + x, c, piece], across, z_slot + 2 * c + piece)
    own_sib = [push(x_block(piece), rows.at[x, c, piece], sibling) for piece in (0, 1)]
    for made in own:
        made.wait()
    for made in own_sib:
        made.wait_recv()

    mine = jnp.where(home, x, 4 + x)

    def gram_block(i):
        xp = around(x, SHIFTS[i])
        product = lax.dot_general(
            rows[mine].reshape(block, width), rows[xp].reshape(block, width),
            (((1,), (1,)), ((), ())), preferred_element_type=jnp.float32,
        )
        part[i] = (product * (1.0 / n_cols)).astype(jnp.bfloat16).reshape(4, quarter, block)

    head, tail = pl.ds(0, half_q), pl.ds(half_q, half_q)
    parts = {}
    for i in range(4):
        parts[i] = [copy(part.at[i, to], pgot.at[i, k], at(y_to=to)) for k, to in enumerate((opposite, up, down))]
        pending.extend(parts[i])

    def gram_send(i):
        for made in parts[i]:
            made.start()

    @pl.when(home)
    def _():
        gram_block(0)
        gram_send(0)

    sib = {}
    far = [None, None]
    from_left[0].wait_recv()
    far[0] = push(rows.at[xl, c, 0], rows.at[xl, c, 0], right)
    sib[(3, 0)] = push(rows.at[xl, c, 0], rows.at[xl, c, 0], sibling)
    from_right[1].wait_recv()
    far[1] = push(rows.at[xr, c, 1], rows.at[xr, c, 1], left)
    sib[(1, 1)] = push(rows.at[xr, c, 1], rows.at[xr, c, 1], sibling)
    from_left[1].wait_recv()
    sib[(3, 1)] = push(rows.at[xl, c, 1], rows.at[xl, c, 1], sibling)
    from_right[0].wait_recv()
    sib[(1, 0)] = push(rows.at[xr, c, 0], rows.at[xr, c, 0], sibling)
    later_z = [push(rows.at[xp, c, piece], rows.at[4 + xp, c, piece], beyond) for xp, piece in ((xl, 0), (xr, 1))]
    to_home = [copy(rows.at[4 + x], rows.at[4 + x], sibling)]

    @pl.when(visitor)
    def _():
        for k in range(4):
            arrive(rows.at[4 + x, k // 2, k % 2], z_slot + k)
        gram_block(0)
        gram_send(0)

    for i in (1, 2):
        for piece in (0, 1):
            sib[(SHIFTS[i], piece)].wait_recv()
        gram_block(i)
        gram_send(i)
    push_if(visitor, to_home)
    to_right, to_left, gsib, gfar, direct_far = {}, {}, [], [], []
    zg_slot = slots(8)

    def total_block(i):
        for made in parts[i]:
            made.wait_recv()
        xp = around(x, SHIFTS[i])
        total = part[i, y].astype(jnp.float32)
        for k in range(3):
            total += pgot[i, k].astype(jnp.float32)
        g32[xp] = total
        gram[xp, x, c] = total.astype(jnp.bfloat16)
        ref = gram.at[xp, x, c]
        if i >= 2:
            direct_far.append(push(ref, ref, at(x_to=xo)))
        to_right[i] = push(ref, ref, right)
        to_left[i] = push(ref, ref, left)
        if i == 0:
            push(ref, gram.at[4, x, c], across, zg_slot + c)
        gsib.append(push(ref, ref, sibling))

    def pass_on(i):
        for made, xs, onward, low, shift in ((to_right[i], xl, right, 0, 1), (to_left[i], xr, left, half_q, 3)):
            made.wait_recv()
            xp = around(xs, SHIFTS[i])
            ref = gram.at[xp, xs, c]
            if i < 2:
                ahead = gram.at[xp, xs, c, pl.ds(low, half_q)]
                gfar.append((i, low, push(ahead, ahead, onward)))
            if SHIFTS[i] == shift:
                push(ref, gram.at[4, xs, c], across, zg_slot + 2 * i + c)
            gsib.append(push(ref, ref, sibling))

    total_block(0)
    total_block(1)
    for piece in (0, 1):
        far[piece].wait_recv()
        sib[(2, piece)] = push(rows.at[xo, c, piece], rows.at[xo, c, piece], sibling)
    for piece in (0, 1):
        sib[(2, piece)].wait_recv()
    gram_block(3)
    gram_send(3)

    total_block(2)
    pass_on(0)
    pass_on(1)
    total_block(3)
    pass_on(2)
    for i, low, made in gfar:
        made.wait_recv()
        ref = gram.at[around(xo, SHIFTS[i]), xo, c, pl.ds(low, half_q)]
        gsib.append(push(ref, ref, sibling))
    pass_on(3)
    direct_far[0].wait_recv()
    ref = gram.at[xr, xo, c]
    gsib.append(push(ref, ref, sibling))
    direct_far[1].wait_recv()
    ref = gram.at[x, xo, c]
    push(ref, gram.at[4, xo, c], across, zg_slot + 6 + c)
    gsib.append(push(ref, ref, sibling))

    sides = ((1, xl, right, 0), (0, xr, left, 1))
    later_x = [copy(rows.at[4 + x, :, p], rows.at[4 + x, :, p], device) for p, _, device, _ in sides]
    later_far = [copy(rows.at[4 + xs, q, p], rows.at[4 + xs, q, p], device) for p, xs, device, q in sides]
    later_home = [copy(rows.at[4 + xs, :, p], rows.at[4 + xs, :, p], sibling) for p, xs, _, _ in sides]
    last_home = [copy(rows.at[4 + xo, q, p], rows.at[4 + xo, q, p], sibling) for p, _, _, q in sides]
    push_if(visitor, later_x)
    last_z = push(rows.at[xo, c, c], rows.at[4 + xo, c, c], beyond)

    for made in gsib:
        made.wait_recv()

    @pl.when(visitor)
    def _():
        for k in range(8):
            arrive(gram.at[0, 0, 0], zg_slot + k)

    first = gram[mine - jnp.where(home, 0, x)].reshape(2 * block, block).T
    for xp in range(4):
        sq[:, :, :, xp * block:(xp + 1) * block] = jnp.dot(
            first, gram[xp].reshape(2 * block, block), preferred_element_type=jnp.float32
        ).astype(jnp.bfloat16).reshape(4, CHUNKS, chunk, block)

    later_sib = []
    for (xp, piece), made in zip(((xl, 0), (xr, 1)), later_z):
        made.wait_recv()
        later_sib.append(push(rows.at[4 + xp, c, piece], rows.at[4 + xp, c, piece], sibling))

    lane = (slice(None), pl.ds(0, 2 * block)), (slice(None), pl.ds(2 * block, 2 * block))
    relay, direct, summed = {}, {}, {}

    def scatter(k):
        relay[k] = [
            push(sq.at[opposite, k, *lane[1]], srel.at[k, 0], to_up),
            push(sq.at[opposite, k, *lane[0]], srel.at[k, 1], to_down),
        ]
        direct[k] = [
            push(sq.at[up, k, *lane[0]], sgot.at[k, 0], to_up),
            push(sq.at[down, k, *lane[1]], sgot.at[k, 1], to_down),
        ]

    def add_on(k):
        summed[k] = []
        for d, (target, device) in enumerate(((up, to_up), (down, to_down))):
            relay[k][d].wait_recv()
            own_part = sq[target, k, :, 2 * block * (1 - d):2 * block * (2 - d)]
            sacc[k, d] = (srel[k, d].astype(jnp.float32) + own_part.astype(jnp.float32)).astype(jnp.bfloat16)
            summed[k].append(push(sacc.at[k, d], sgot.at[k, 2 + d], device))

    near = (slice(None), pl.ds(0, 4 * block))
    other = (slice(None), pl.ds(4 * block, 4 * block))
    takes = c == taker
    takes_down, takes_up, takes_opposite = c == down // 2, c == up // 2, c == opposite // 2
    both = jnp.logical_and
    spread, onward, leaving = {}, {}, []

    def mix(k):
        for made in direct[k] + summed[k]:
            made.wait_recv()
        total = sq[y, k].astype(jnp.float32) + jnp.concatenate(
            [sgot[k, 0].astype(jnp.float32) + sgot[k, 3].astype(jnp.float32),
             sgot[k, 1].astype(jnp.float32) + sgot[k, 2].astype(jnp.float32)], axis=1)
        g = jnp.concatenate([g32[xp, k * chunk:(k + 1) * chunk, :] for xp in range(4)], axis=1)
        value = (CUBIC * g + QUINTIC * total).astype(jnp.bfloat16)
        mloc[k] = value
        src = mloc.at[k]
        spread[k] = dict(
            down_near=copy(src, mixed.at[k, y, *near], at(c_to=taker, y_to=up)),
            up_near=copy(src, mixed.at[k, y, *near], at(c_to=taker, y_to=down)),
            own_near=copy(src, mixed.at[k, y, *near], sibling),
            own_other=copy(src, mixed.at[k, y, *other], at(z_to=1 - z, c_to=taker)),
            down_other=copy(src, mixed.at[k, y, *other], at(z_to=1 - z, c_to=taker, y_to=up)),
            up_other=copy(src, mixed.at[k, y, *other], at(z_to=1 - z, c_to=taker, y_to=down)),
        )
        push_if(visitor, [spread[k][name] for name in ("up_other", "down_other", "own_other")])
        push_if(home, [spread[k]["down_near"], spread[k]["up_near"]])
        push_if(both(home, jnp.logical_not(takes)), [spread[k]["own_near"]])

        @pl.when(both(home, takes))
        def _():
            mixed[k, y, :, :4 * block] = value

    def carry(k):
        arrive_if(takes_down, [spread[k]["down_near"]])
        ref = mixed.at[k, down, *near]
        onward[k] = {}
        onward[k]["far_near"] = copy(ref, ref, to_up)
        push_if(takes_down, [onward[k]["far_near"]])
        arrive_if(takes_up, [spread[k]["up_other"]])
        ref = mixed.at[k, up, *other]
        onward[k]["far_other"] = copy(ref, ref, to_down)
        push_if(takes_up, [onward[k]["far_other"]])

    def multiply(k):
        arrive_if(takes_down, [spread[k]["down_other"]])
        arrive_if(takes_up, [spread[k]["up_near"]])
        arrive_if(takes_opposite, [onward[k]["far_near"], onward[k]["far_other"]])
        arrive_if(both(takes, visitor), [spread[k]["own_near"]])
        arrive_if(takes, [spread[k]["own_other"]])
        lhs = mixed[k, pl.ds(2 * c, 2)].reshape(2 * chunk, 8 * block)
        tile = width // 4
        for t in range(4):
            cols = slice(t * tile, (t + 1) * tile)
            product = jnp.dot(
                lhs, rows[:, :, :, :, cols].reshape(8 * block, tile), preferred_element_type=jnp.float32
            )
            for q in range(2):
                low = q * quarter + k * chunk
                result[low:low + chunk, cols] = (
                    LINEAR * rows[x, c, q, k * chunk:(k + 1) * chunk, cols].astype(jnp.float32)
                    + product[q * chunk:(q + 1) * chunk]
                ).astype(jnp.bfloat16)
        for q in range(2):
            done = pl.ds(q * quarter + k * chunk, chunk)
            made = pltpu.make_async_copy(result.at[done, :], o_ref.at[done, :], lsem.at[2 + 2 * k + q])
            made.start()
            leaving.append(made)

    def pass_rows():
        for p in range(2):
            arrive_if(visitor, [later_x[p]])
            push_if(visitor, [later_far[p], later_home[p]])
        last_z.wait_recv()
        later_sib.append(push(rows.at[4 + xo, c, c], rows.at[4 + xo, c, c], sibling))

    def end_rows():
        for p in range(2):
            arrive_if(visitor, [later_far[p]])
            push_if(visitor, [last_home[p]])
        for made in later_sib:
            made.wait_recv()
        arrive_if(home, to_home + later_home + last_home)

    stages = (
        (scatter, 0), (add_on, AHEAD), (mix, AHEAD + 1), (carry, AHEAD + 2),
        (multiply, AHEAD + 3 + HOLD),
    )
    for slot in range(CHUNKS + AHEAD + 3 + HOLD):
        if slot == PASS_AT:
            pass_rows()
        for stage, delay in stages:
            if stage is multiply and slot == delay:
                end_rows()
            if 0 <= slot - delay < CHUNKS:
                stage(slot - delay)

    for made in leaving:
        made.wait()
    for made in pending:
        made.wait_send()
    for condition, copies in guarded:

        @pl.when(condition)
        def _():
            for made in copies:
                made.wait_send()


def body(n_cols, iterate):
    height, width = iterate.shape
    half = height // 2
    block = 2 * height
    chunk = half // CHUNKS
    bf16 = jnp.bfloat16
    return pl.pallas_call(
        functools.partial(kernel, n_cols),
        out_shape=jax.ShapeDtypeStruct(iterate.shape, bf16),
        in_specs=[pl.BlockSpec(memory_space=pl.ANY)],
        out_specs=pl.BlockSpec(memory_space=pl.ANY),
        scratch_shapes=[
            pltpu.VMEM((8, 2, 2, half, width), bf16),
            pltpu.VMEM((4, 4, half, block), bf16),
            pltpu.VMEM((4, 3, half, block), bf16),
            pltpu.VMEM((5, 4, 2, half, block), bf16),
            pltpu.VMEM((4, half, block), jnp.float32),
            pltpu.VMEM((4, CHUNKS, chunk, 4 * block), bf16),
            pltpu.VMEM((CHUNKS, 2, chunk, 2 * block), bf16),
            pltpu.VMEM((CHUNKS, 2, chunk, 2 * block), bf16),
            pltpu.VMEM((CHUNKS, 4, chunk, 2 * block), bf16),
            pltpu.VMEM((CHUNKS, chunk, 4 * block), bf16),
            pltpu.VMEM((CHUNKS, 4, chunk, 8 * block), bf16),
            pltpu.VMEM(iterate.shape, bf16),
            pltpu.SemaphoreType.DMA((256,)),
            pltpu.SemaphoreType.DMA((256,)),
            pltpu.SemaphoreType.DMA((2 + 2 * CHUNKS,)),
        ],
        compiler_params=pltpu.CompilerParams(
            collective_id=0, has_side_effects=True, vmem_limit_bytes=60 * 2**20
        ),
        cost_estimate=pl.CostEstimate(flops=6 * 10**9, bytes_accessed=2 * 10**6, transcendentals=0),
        name="newton_schulz",
    )(iterate)


def solution(mesh):
    spec = P(("expert", "grid"), "layer")

    def run(iterate):
        step = functools.partial(body, iterate.shape[1])
        return jax.shard_map(step, mesh=mesh, in_specs=(spec,), out_specs=spec, check_vma=False)(iterate)

    return run
```

```python
import functools

import jax
import jax.numpy as jnp
from jax import lax
from jax.experimental import pallas as pl
from jax.experimental.pallas import tpu as pltpu
from jax.sharding import PartitionSpec as P

MESH = pl.DeviceIdType.MESH

LINEAR = 3.4445
CUBIC = -4.775
QUINTIC = 2.0315

SHIFTS = (0, 1, 3, 2)
CHUNKS = 2
AHEAD = 1
HOLD = 0
PASS_AT = 3


def kernel(
    n_cols, x_ref, o_ref, rows, part, pgot, gram, g32, sq, srel, sacc, sgot, mloc, mixed, result, ssem, rsem, lsem
):
    half, width = x_ref.shape[0] // 2, x_ref.shape[1]
    quarter = half
    half_q = quarter // 2
    chunk = quarter // CHUNKS
    block = 4 * half
    expert, grid, y = lax.axis_index("expert"), lax.axis_index("grid"), lax.axis_index("layer")
    x, z, c = grid // 4, (grid // 2) % 2, grid % 2
    home = c == z
    visitor = jnp.logical_not(home)

    def at(x_to=None, z_to=None, c_to=None, y_to=None):
        gx = x if x_to is None else x_to
        gz = z if z_to is None else z_to
        gc = c if c_to is None else c_to
        return (expert, gx * 4 + gz * 2 + gc, y if y_to is None else y_to)

    def around(base, step):
        return (base + step) % 4

    up, down, opposite = around(y, 1), around(y, 3), around(y, 2)
    xl, xr, xo = around(x, 3), around(x, 1), around(x, 2)
    right, left = at(x_to=xr), at(x_to=xl)
    sibling = at(c_to=1 - c)
    beyond = at(z_to=1 - z)
    across = at(z_to=1 - z, c_to=z)
    to_up, to_down = at(y_to=up), at(y_to=down)
    taker = y // 2

    def x_block(core_half):
        return x_ref.at[pl.ds(core_half * half, half), :]

    own = [pltpu.make_async_copy(x_block(piece), rows.at[x, c, piece], lsem.at[piece]) for piece in (0, 1)]
    for made in own:
        made.start()

    barrier = pltpu.get_barrier_semaphore()
    greeted = [right, left, sibling, beyond, at(z_to=1 - z, c_to=1 - c), to_up, to_down]
    greeted += [at(c_to=1 - c, y_to=up), at(c_to=1 - c, y_to=down), at(y_to=opposite), at(x_to=xo)]
    greeted += [at(z_to=1 - z, c_to=core, y_to=to) for core in (0, 1) for to in (up, down)]
    for device in greeted:
        pl.semaphore_signal(barrier, inc=1, device_id=device, device_id_type=MESH)
    pl.semaphore_wait(barrier, len(greeted))

    used = [0, 0]
    pending = []
    guarded = []

    def slots(count=1):
        used[1] += count
        return used[1] - count

    def copy(src, dst, device, slot=None):
        used[0] += 1
        return pltpu.make_async_remote_copy(
            src_ref=src, dst_ref=dst, send_sem=ssem.at[used[0] - 1],
            recv_sem=rsem.at[slots() if slot is None else slot], device_id=device, device_id_type=MESH,
        )

    def push(src, dst, device, slot=None):
        made = copy(src, dst, device, slot)
        made.start()
        pending.append(made)
        return made

    def push_if(condition, copies):
        guarded.append((condition, copies))

        @pl.when(condition)
        def _():
            for made in copies:
                made.start()

    def arrive(ref, slot):
        pltpu.make_async_remote_copy(
            src_ref=ref, dst_ref=ref, send_sem=ssem.at[0], recv_sem=rsem.at[slot],
            device_id=sibling, device_id_type=MESH,
        ).wait_recv()

    def arrive_if(condition, copies):
        @pl.when(condition)
        def _():
            for made in copies:
                made.wait_recv()

    from_left = [None, None]
    from_right = [None, None]
    for piece in (0, 1):
        from_left[piece] = push(x_block(piece), rows.at[x, c, piece], right)
        from_right[1 - piece] = push(x_block(1 - piece), rows.at[x, c, 1 - piece], left)
    z_slot = slots(4)
    for piece in (0, 1):
        push(x_block(piece), rows.at[4 + x, c, piece], across, z_slot + 2 * c + piece)
    own_sib = [push(x_block(piece), rows.at[x, c, piece], sibling) for piece in (0, 1)]
    for made in own:
        made.wait()
    for made in own_sib:
        made.wait_recv()

    mine = jnp.where(home, x, 4 + x)

    def gram_block(i):
        xp = around(x, SHIFTS[i])
        product = lax.dot_general(
            rows[mine].reshape(block, width), rows[xp].reshape(block, width),
            (((1,), (1,)), ((), ())), preferred_element_type=jnp.float32,
        )
        part[i] = (product * (1.0 / n_cols)).astype(jnp.bfloat16).reshape(4, quarter, block)

    head, tail = pl.ds(0, half_q), pl.ds(half_q, half_q)
    parts = {}
    for i in range(4):
        parts[i] = [copy(part.at[i, to], pgot.at[i, k], at(y_to=to)) for k, to in enumerate((opposite, up, down))]
        pending.extend(parts[i])

    def gram_send(i):
        for made in parts[i]:
            made.start()

    @pl.when(home)
    def _():
        gram_block(0)
        gram_send(0)

    sib = {}
    far = [None, None]
    from_left[0].wait_recv()
    far[0] = push(rows.at[xl, c, 0], rows.at[xl, c, 0], right)
    sib[(3, 0)] = push(rows.at[xl, c, 0], rows.at[xl, c, 0], sibling)
    from_right[1].wait_recv()
    far[1] = push(rows.at[xr, c, 1], rows.at[xr, c, 1], left)
    sib[(1, 1)] = push(rows.at[xr, c, 1], rows.at[xr, c, 1], sibling)
    from_left[1].wait_recv()
    sib[(3, 1)] = push(rows.at[xl, c, 1], rows.at[xl, c, 1], sibling)
    from_right[0].wait_recv()
    sib[(1, 0)] = push(rows.at[xr, c, 0], rows.at[xr, c, 0], sibling)
    later_z = [push(rows.at[xp, c, piece], rows.at[4 + xp, c, piece], beyond) for xp, piece in ((xl, 0), (xr, 1))]
    to_home = [copy(rows.at[4 + x], rows.at[4 + x], sibling)]

    @pl.when(visitor)
    def _():
        for k in range(4):
            arrive(rows.at[4 + x, k // 2, k % 2], z_slot + k)
        gram_block(0)
        gram_send(0)

    for i in (1, 2):
        for piece in (0, 1):
            sib[(SHIFTS[i], piece)].wait_recv()
        gram_block(i)
        gram_send(i)
    to_right, to_left, gsib, gfar, direct_far = {}, {}, [], [], []
    zg_slot = slots(8)

    def total_block(i):
        for made in parts[i]:
            made.wait_recv()
        xp = around(x, SHIFTS[i])
        total = part[i, y].astype(jnp.float32)
        for k in range(3):
            total += pgot[i, k].astype(jnp.float32)
        g32[xp] = total
        gram[xp, x, c] = total.astype(jnp.bfloat16)
        ref = gram.at[xp, x, c]
        if i >= 2:
            direct_far.append(push(ref, ref, at(x_to=xo)))
        to_right[i] = push(ref, ref, right)
        to_left[i] = push(ref, ref, left)
        if i == 0:
            push(ref, gram.at[4, x, c], across, zg_slot + c)
        gsib.append(push(ref, ref, sibling))

    def pass_on(i):
        for made, xs, onward, low, shift in ((to_right[i], xl, right, 0, 1), (to_left[i], xr, left, half_q, 3)):
            made.wait_recv()
            xp = around(xs, SHIFTS[i])
            ref = gram.at[xp, xs, c]
            if i < 2:
                ahead = gram.at[xp, xs, c, pl.ds(low, half_q)]
                gfar.append((i, low, push(ahead, ahead, onward)))
            if SHIFTS[i] == shift:
                push(ref, gram.at[4, xs, c], across, zg_slot + 2 * i + c)
            gsib.append(push(ref, ref, sibling))

    total_block(0)
    total_block(1)
    for piece in (0, 1):
        far[piece].wait_recv()
        sib[(2, piece)] = push(rows.at[xo, c, piece], rows.at[xo, c, piece], sibling)
    for piece in (0, 1):
        sib[(2, piece)].wait_recv()
    gram_block(3)
    gram_send(3)

    total_block(2)
    pass_on(0)
    pass_on(1)
    total_block(3)
    pass_on(2)
    for i, low, made in gfar:
        made.wait_recv()
        ref = gram.at[around(xo, SHIFTS[i]), xo, c, pl.ds(low, half_q)]
        gsib.append(push(ref, ref, sibling))
    pass_on(3)
    direct_far[0].wait_recv()
    ref = gram.at[xr, xo, c]
    gsib.append(push(ref, ref, sibling))
    direct_far[1].wait_recv()
    ref = gram.at[x, xo, c]
    push(ref, gram.at[4, xo, c], across, zg_slot + 6 + c)
    gsib.append(push(ref, ref, sibling))

    sides = ((1, xl, right, 0), (0, xr, left, 1))
    later_x = [copy(rows.at[4 + x, :, p], rows.at[4 + x, :, p], device) for p, _, device, _ in sides]
    later_far = [copy(rows.at[4 + xs, q, p], rows.at[4 + xs, q, p], device) for p, xs, device, q in sides]
    later_home = [copy(rows.at[4 + xs, :, p], rows.at[4 + xs, :, p], sibling) for p, xs, _, _ in sides]
    last_home = [copy(rows.at[4 + xo, q, p], rows.at[4 + xo, q, p], sibling) for p, _, _, q in sides]
    push_if(visitor, later_x + to_home)
    last_z = push(rows.at[xo, c, c], rows.at[4 + xo, c, c], beyond)

    for made in gsib:
        made.wait_recv()

    @pl.when(visitor)
    def _():
        for k in range(8):
            arrive(gram.at[0, 0, 0], zg_slot + k)

    first = gram[mine - jnp.where(home, 0, x)].reshape(2 * block, block).T
    for xp in range(4):
        sq[:, :, :, xp * block:(xp + 1) * block] = jnp.dot(
            first, gram[xp].reshape(2 * block, block), preferred_element_type=jnp.float32
        ).astype(jnp.bfloat16).reshape(4, CHUNKS, chunk, block)

    later_sib = []
    for (xp, piece), made in zip(((xl, 0), (xr, 1)), later_z):
        made.wait_recv()
        later_sib.append(push(rows.at[4 + xp, c, piece], rows.at[4 + xp, c, piece], sibling))

    lane = (slice(None), pl.ds(0, 2 * block)), (slice(None), pl.ds(2 * block, 2 * block))
    relay, direct, summed = {}, {}, {}

    def scatter(k):
        relay[k] = [
            push(sq.at[opposite, k, *lane[1]], srel.at[k, 0], to_up),
            push(sq.at[opposite, k, *lane[0]], srel.at[k, 1], to_down),
        ]
        direct[k] = [
            push(sq.at[up, k, *lane[0]], sgot.at[k, 0], to_up),
            push(sq.at[down, k, *lane[1]], sgot.at[k, 1], to_down),
        ]

    def add_on(k):
        summed[k] = []
        for d, (target, device) in enumerate(((up, to_up), (down, to_down))):
            relay[k][d].wait_recv()
            own_part = sq[target, k, :, 2 * block * (1 - d):2 * block * (2 - d)]
            sacc[k, d] = (srel[k, d].astype(jnp.float32) + own_part.astype(jnp.float32)).astype(jnp.bfloat16)
            summed[k].append(push(sacc.at[k, d], sgot.at[k, 2 + d], device))

    near = (slice(None), pl.ds(0, 4 * block))
    other = (slice(None), pl.ds(4 * block, 4 * block))
    takes = c == taker
    takes_down, takes_up, takes_opposite = c == down // 2, c == up // 2, c == opposite // 2
    both = jnp.logical_and
    spread, onward, leaving = {}, {}, []

    def mix(k):
        for made in direct[k] + summed[k]:
            made.wait_recv()
        total = sq[y, k].astype(jnp.float32) + jnp.concatenate(
            [sgot[k, 0].astype(jnp.float32) + sgot[k, 3].astype(jnp.float32),
             sgot[k, 1].astype(jnp.float32) + sgot[k, 2].astype(jnp.float32)], axis=1)
        g = jnp.concatenate([g32[xp, k * chunk:(k + 1) * chunk, :] for xp in range(4)], axis=1)
        value = (CUBIC * g + QUINTIC * total).astype(jnp.bfloat16)
        mloc[k] = value
        src = mloc.at[k]
        spread[k] = dict(
            down_near=copy(src, mixed.at[k, y, *near], at(c_to=taker, y_to=up)),
            up_near=copy(src, mixed.at[k, y, *near], at(c_to=taker, y_to=down)),
            own_near=copy(src, mixed.at[k, y, *near], sibling),
            own_other=copy(src, mixed.at[k, y, *other], at(z_to=1 - z, c_to=taker)),
            down_other=copy(src, mixed.at[k, y, *other], at(z_to=1 - z, c_to=taker, y_to=up)),
            up_other=copy(src, mixed.at[k, y, *other], at(z_to=1 - z, c_to=taker, y_to=down)),
        )
        push_if(visitor, [spread[k][name] for name in ("up_other", "down_other", "own_other")])
        push_if(home, [spread[k]["down_near"], spread[k]["up_near"]])
        push_if(both(home, jnp.logical_not(takes)), [spread[k]["own_near"]])

        @pl.when(both(home, takes))
        def _():
            mixed[k, y, :, :4 * block] = value

    def carry(k):
        arrive_if(takes_down, [spread[k]["down_near"]])
        ref = mixed.at[k, down, *near]
        onward[k] = {}
        onward[k]["far_near"] = copy(ref, ref, to_up)
        push_if(takes_down, [onward[k]["far_near"]])
        arrive_if(takes_up, [spread[k]["up_other"]])
        ref = mixed.at[k, up, *other]
        onward[k]["far_other"] = copy(ref, ref, to_down)
        push_if(takes_up, [onward[k]["far_other"]])

    def multiply(k):
        arrive_if(takes_down, [spread[k]["down_other"]])
        arrive_if(takes_up, [spread[k]["up_near"]])
        arrive_if(takes_opposite, [onward[k]["far_near"], onward[k]["far_other"]])
        arrive_if(both(takes, visitor), [spread[k]["own_near"]])
        arrive_if(takes, [spread[k]["own_other"]])
        lhs = mixed[k, pl.ds(2 * c, 2)].reshape(2 * chunk, 8 * block)
        tile = width // 4
        for t in range(4):
            cols = slice(t * tile, (t + 1) * tile)
            product = jnp.dot(
                lhs, rows[:, :, :, :, cols].reshape(8 * block, tile), preferred_element_type=jnp.float32
            )
            for q in range(2):
                low = q * quarter + k * chunk
                result[low:low + chunk, cols] = (
                    LINEAR * rows[x, c, q, k * chunk:(k + 1) * chunk, cols].astype(jnp.float32)
                    + product[q * chunk:(q + 1) * chunk]
                ).astype(jnp.bfloat16)
        for q in range(2):
            done = pl.ds(q * quarter + k * chunk, chunk)
            made = pltpu.make_async_copy(result.at[done, :], o_ref.at[done, :], lsem.at[2 + 2 * k + q])
            made.start()
            leaving.append(made)

    def pass_rows():
        for p in range(2):
            arrive_if(visitor, [later_x[p]])
            push_if(visitor, [later_far[p], later_home[p]])
        last_z.wait_recv()
        later_sib.append(push(rows.at[4 + xo, c, c], rows.at[4 + xo, c, c], sibling))

    def end_rows():
        for p in range(2):
            arrive_if(visitor, [later_far[p]])
            push_if(visitor, [last_home[p]])
        for made in later_sib:
            made.wait_recv()
        arrive_if(home, to_home + later_home + last_home)

    stages = (
        (scatter, 0), (add_on, AHEAD), (mix, AHEAD + 1), (carry, AHEAD + 2),
        (multiply, AHEAD + 3 + HOLD),
    )
    for slot in range(CHUNKS + AHEAD + 3 + HOLD):
        if slot == PASS_AT:
            pass_rows()
        for stage, delay in stages:
            if stage is multiply and slot == delay:
                end_rows()
            if 0 <= slot - delay < CHUNKS:
                stage(slot - delay)

    for made in leaving:
        made.wait()
    for made in pending:
        made.wait_send()
    for condition, copies in guarded:

        @pl.when(condition)
        def _():
            for made in copies:
                made.wait_send()


def body(n_cols, iterate):
    height, width = iterate.shape
    half = height // 2
    block = 2 * height
    chunk = half // CHUNKS
    bf16 = jnp.bfloat16
    return pl.pallas_call(
        functools.partial(kernel, n_cols),
        out_shape=jax.ShapeDtypeStruct(iterate.shape, bf16),
        in_specs=[pl.BlockSpec(memory_space=pl.ANY)],
        out_specs=pl.BlockSpec(memory_space=pl.ANY),
        scratch_shapes=[
            pltpu.VMEM((8, 2, 2, half, width), bf16),
            pltpu.VMEM((4, 4, half, block), bf16),
            pltpu.VMEM((4, 3, half, block), bf16),
            pltpu.VMEM((5, 4, 2, half, block), bf16),
            pltpu.VMEM((4, half, block), jnp.float32),
            pltpu.VMEM((4, CHUNKS, chunk, 4 * block), bf16),
            pltpu.VMEM((CHUNKS, 2, chunk, 2 * block), bf16),
            pltpu.VMEM((CHUNKS, 2, chunk, 2 * block), bf16),
            pltpu.VMEM((CHUNKS, 4, chunk, 2 * block), bf16),
            pltpu.VMEM((CHUNKS, chunk, 4 * block), bf16),
            pltpu.VMEM((CHUNKS, 4, chunk, 8 * block), bf16),
            pltpu.VMEM(iterate.shape, bf16),
            pltpu.SemaphoreType.DMA((256,)),
            pltpu.SemaphoreType.DMA((256,)),
            pltpu.SemaphoreType.DMA((2 + 2 * CHUNKS,)),
        ],
        compiler_params=pltpu.CompilerParams(
            collective_id=0, has_side_effects=True, vmem_limit_bytes=60 * 2**20
        ),
        cost_estimate=pl.CostEstimate(flops=6 * 10**9, bytes_accessed=2 * 10**6, transcendentals=0),
        name="newton_schulz",
    )(iterate)


def solution(mesh):
    spec = P(("expert", "grid"), "layer")

    def run(iterate):
        step = functools.partial(body, iterate.shape[1])
        return jax.shard_map(step, mesh=mesh, in_specs=(spec,), out_specs=spec, check_vma=False)(iterate)

    return run
```
